256 devices in a mesh: dp: 4 (over x), wide: 64 (over y, z, core).
Axes of the slice: x: 4, y: 4, z: 8, core: 2. Of those that a mesh axis runs over, the one named last changes fastest.
Arguments:
- clips: bfloat16 [4, 64, 4, 128, 512], P('dp', 'wide'), may hold values from -8 to 8
- w_spatial: bfloat16 [4608, 512], P(None, 'dp'), may hold values from -0.09375 to 0.09375
- w_time: bfloat16 [1536, 512], replicated, may hold values from -0.15625 to 0.15625
- norm_gain: float32 [512], replicated, may hold values from 0.1 to 1.9
- norm_bias: float32 [512], replicated, may hold values from -0.6 to 0.6
- grad_out: bfloat16 [4, 64, 512, 512], P('dp', None, 'wide'), may hold values from -16 to 16
Outputs:
- grad_clips: bfloat16 [4, 64, 4, 128, 512], P('dp', 'wide')
- spatial_grad: float32 [4608, 512], P('dp', 'wide')
- time_grad: float32 [1536, 512], P('dp', 'wide')
The draws below stay inside these ranges and needn't reach their ends.
All inputs are finite; a program needn't handle non-finite values.
Results may differ from the reference program's by a relative error of at most 0.009.
Values may be sent and summed in bfloat16 or wider, within the bound.
A program may use at most 128 MiB of HBM per device.

```python
import jax
import jax.numpy as jnp
from jax import lax

C = 512
G = 32
HS = 4
WS = 128
FRAMES = 8
CL_GROUP = 8
CLIPS = 32
PIX = 512
N_DP = 4


def draw_clips(key, part):
    shape = (N_DP, CL_GROUP * FRAMES, HS, WS, C)
    noise = jax.random.normal(jax.random.fold_in(key, 11), shape, jnp.float32)
    values = noise
    return jnp.clip(values, -8.0, 8.0).astype(jnp.bfloat16)


def strengthened(entries, own_key, source, target, blocks, factor):
    owner, partner = [(jnp.arange(entries.shape[position]) // (entries.shape[position] // blocks)).reshape([-1 if axis == position else 1 for axis in range(entries.ndim)]) for position in (source, target)]
    chosen = jax.random.permutation(own_key, blocks)[partner]
    strong = (owner == chosen) | (owner == (partner + blocks // 2) % blocks)
    return jnp.where(strong, factor * entries, entries)


def steps_of(stream_key, extent, cuts, smallest, largest):
    factor_of = 1.0
    for position, shards_of in cuts:
        draws = jax.random.uniform(jax.random.fold_in(jax.random.fold_in(stream_key, 6), position), (shards_of,), jnp.float32, smallest / len(cuts), largest / len(cuts))
        factor_of = factor_of * jnp.repeat(jnp.exp(draws), extent[position] // shards_of).reshape((-1,) + (1,) * (len(extent) - 1 - position))
    return factor_of


def normal_values(rng, shape, spread, reach, pieces=(), held_as=jnp.bfloat16):
    result = spread * jax.random.normal(rng, shape, jnp.float32)
    if pieces:
        result = result * steps_of(rng, shape, pieces, -0.22, 0.18)
    return jnp.clip(result, -reach, reach).astype(held_as)


def gaussian_with(stream_key, dims, spread, most, shards, heavy, dtype=jnp.bfloat16):
    entries = spread * jax.random.normal(stream_key, dims, jnp.float32)
    if shards:
        entries = entries * steps_of(stream_key, dims, shards, -0.22, 0.18)
    return jnp.clip(strengthened(entries, jax.random.fold_in(stream_key, 3), *heavy), -most, most).astype(dtype)


def setup_inputs(seed: int = 0) -> dict:
    keys = jax.random.split(jax.random.key(seed), 7)
    clips = draw_clips(jax.random.fold_in(keys[6], 71), 0)
    w_spatial = normal_values(keys[1], (9 * C, C), (9 * C) ** -0.5, 0.09375, ((1, 4),))
    w_time = normal_values(keys[2], (3 * C, C), (3 * C) ** -0.5, 0.15625)
    norm_gain = jnp.clip(1.0 + 0.18 * jax.random.normal(keys[3], (C,), jnp.float32), 0.1, 1.9)
    norm_bias = jnp.clip(jax.random.uniform(keys[4], (C,), jnp.float32, -0.6, 0.6), -0.6, 0.6)
    grad_out = gaussian_with(keys[5], (N_DP, CL_GROUP * FRAMES, PIX, C), 1.0, 16.0, ((0, 4), (2, 64)), (2, 3, 64, 4.0))
    return {"clips": clips, "w_spatial": w_spatial, "w_time": w_time, "norm_gain": norm_gain, "norm_bias": norm_bias, "grad_out": grad_out}


EPSILON = 1e-06
CONTRACT_ROWS = (((0,), (0,)), ((), ()))
CONTRACT_COLS = (((1,), (1,)), ((), ()))

def pad_frames(frames):
    return jnp.pad(frames, ((0, 0), (1, 1), (1, 1), (0, 0)))

def spatial_forward(frames, weights):
    frame_total, row_count, col_count, chan_count = frames.shape
    padded = pad_frames(frames)
    accum_out = jnp.zeros((frame_total * row_count * col_count, weights.shape[1]), jnp.float32)
    for tap_index in range(9):
        row_off, col_off = (tap_index // 3, tap_index % 3)
        window = padded[:, row_off:row_off + row_count, col_off:col_off + col_count, :].reshape(-1, chan_count)
        tap_weight = weights[tap_index * chan_count:(tap_index + 1) * chan_count]
        accum_out = accum_out + jnp.dot(window, tap_weight, preferred_element_type=jnp.float32)
    return accum_out.reshape(frame_total, row_count, col_count, -1)

def spatial_backward(frames, grad_hidden, weights):
    frame_total, row_count, col_count, chan_count = frames.shape
    padded_in = pad_frames(frames)
    padded_grad = pad_frames(grad_hidden)
    grad_flat = grad_hidden.reshape(-1, chan_count)
    grad_input = jnp.zeros((frame_total * row_count * col_count, chan_count), jnp.float32)
    tap_grads = []
    for tap_index in range(9):
        row_off, col_off = (tap_index // 3, tap_index % 3)
        window = padded_in[:, row_off:row_off + row_count, col_off:col_off + col_count, :].reshape(-1, chan_count)
        tap_grads.append(lax.dot_general(window, grad_flat, CONTRACT_ROWS, preferred_element_type=jnp.float32))
        flipped = padded_grad[:, 2 - row_off:2 - row_off + row_count, 2 - col_off:2 - col_off + col_count, :].reshape(-1, chan_count)
        tap_weight = weights[tap_index * chan_count:(tap_index + 1) * chan_count]
        grad_input = grad_input + lax.dot_general(flipped, tap_weight, CONTRACT_COLS, preferred_element_type=jnp.float32)
    return (grad_input.reshape(frames.shape), jnp.concatenate(tap_grads, axis=0))

def norm_forward(hidden, norm_gain, norm_bias):
    frame_total, row_count, col_count, chan_count = hidden.shape
    grouped = hidden.astype(jnp.float32).reshape(frame_total, row_count * col_count, G, chan_count // G)
    group_mean = lax.optimization_barrier(jnp.mean(grouped, axis=(1, 3), keepdims=True))
    centered = grouped - group_mean
    variance = lax.optimization_barrier(jnp.mean(centered * centered, axis=(1, 3), keepdims=True))
    inv_std = lax.rsqrt(variance + EPSILON)
    normed = centered * inv_std
    preact = normed.reshape(hidden.shape) * norm_gain + norm_bias
    return (preact, normed, inv_std)

def norm_backward(grad_act, preact, normed, inv_std, norm_gain):
    sigmoid_z = jax.nn.sigmoid(preact)
    grad_pre = grad_act.astype(jnp.float32) * sigmoid_z * (1.0 + preact * (1.0 - sigmoid_z))
    grad_normed = (grad_pre * norm_gain).reshape(normed.shape)
    mean_grad = lax.optimization_barrier(jnp.mean(grad_normed, axis=(1, 3), keepdims=True))
    mean_proj = lax.optimization_barrier(jnp.mean(grad_normed * normed, axis=(1, 3), keepdims=True))
    return ((grad_normed - mean_grad - normed * mean_proj) * inv_std).reshape(preact.shape)

def temporal_backward(tiles, grad_out, w_time):
    clip_count, frame_total, pix_count, chan_count = tiles.shape
    grad_act = jnp.zeros(tiles.shape, jnp.float32)
    tap_grads = []
    for tap_index in range(3):
        kept = frame_total - tap_index
        earlier = tiles[:, :kept].reshape(-1, chan_count)
        later = grad_out[:, tap_index:].reshape(-1, chan_count)
        tap_grads.append(lax.dot_general(earlier, later, CONTRACT_ROWS, preferred_element_type=jnp.float32))
        tap_weight = w_time[tap_index * chan_count:(tap_index + 1) * chan_count]
        back_part = lax.dot_general(later, tap_weight, CONTRACT_COLS, preferred_element_type=jnp.float32)
        back_part = back_part.reshape(clip_count, kept, pix_count, chan_count)
        grad_act = grad_act + jnp.pad(back_part, ((0, 0), (0, tap_index), (0, 0), (0, 0)))
    return (jnp.concatenate(tap_grads, axis=0), grad_act)

def reference(clips, w_spatial, w_time, norm_gain, norm_bias, grad_out):
    frames = clips.reshape(-1, HS, WS, C)
    hidden = spatial_forward(frames, w_spatial).astype(jnp.bfloat16)
    preact, normed, inv_std = norm_forward(hidden, norm_gain, norm_bias)
    act = jax.nn.silu(preact).astype(jnp.bfloat16)
    tiles = act.reshape(CLIPS, FRAMES, HS * WS, C)
    time_raw, grad_act = temporal_backward(tiles, grad_out.reshape(CLIPS, FRAMES, HS * WS, C), w_time)
    grad_act = grad_act.astype(jnp.bfloat16).reshape(frames.shape)
    grad_hidden = norm_backward(grad_act, preact, normed, inv_std, norm_gain).astype(jnp.bfloat16)
    grad_input, spatial_raw = spatial_backward(frames, grad_hidden, w_spatial)
    grad_scale = float(CLIPS * FRAMES * HS * WS) ** (-0.5)
    return (grad_input.astype(jnp.bfloat16).reshape(clips.shape), spatial_raw * grad_scale, time_raw * grad_scale)
```

```python
import jax
import jax.numpy as jnp
from jax import lax
from jax.experimental import pallas as pl
from jax.experimental.pallas import tpu as pltpu
from jax.sharding import PartitionSpec as P

MESH = pl.DeviceIdType.MESH
F32 = jnp.float32
BF16 = jnp.bfloat16
EPSILON = 1e-06
CONTRACT_COLS = (((1,), (1,)), ((), ()))
NX, NY, NZ = 4, 4, 8
C = 512
PIX = 512
TAP_ROWS = 4608
HALF = TAP_ROWS // 2
PIECES = 3
PIECE = HALF // PIECES


def place():
    x = lax.axis_index("dp")
    w = lax.axis_index("wide")
    return x, w, w // 16, (w // 2) % 8, w % 2


def greet(partners):
    barrier = pltpu.get_barrier_semaphore()
    for partner in partners:
        pl.semaphore_signal(barrier, inc=1, device_id=partner, device_id_type=MESH)
    pl.semaphore_wait(barrier, len(partners))


def gather_kernel(
    w_ref, go_ref, w_out, go_out, slots,
    w_send, w_recv, f_send, f_recv, s_send, s_recv, y_send, y_recv, z_send, z_recv, e_send, e_recv, local_sem,
):
    x, w, y, z, c = place()
    way = 1 - 2 * c
    sibling = (x, w + way)
    ahead = (lax.rem(x + way + NX, NX), w)
    behind = (lax.rem(x - way + NX, NX), w)
    base = y * 16
    spot = lax.rem(w, 16)

    def ring_y(j):
        return (x, lax.rem(y + j, NY) * 16 + spot)

    def ring_z(k):
        return (x, base + lax.rem(spot + k, 16))

    greet([ahead, behind] + [ring_y(j) for j in range(1, NY)] + [ring_z(k) for k in range(1, 16)])

    def copy(src, dst, send, recv, target):
        return pltpu.make_async_remote_copy(
            src_ref=src, dst_ref=dst, send_sem=send, recv_sem=recv, device_id=target, device_id_type=MESH
        )

    def y_copy(j):
        frames = pl.ds(lax.rem(y + j, NY) * 16, 16)
        return copy(go_ref.at[frames], slots.at[j - 1], y_send.at[j - 1], y_recv.at[j - 1], ring_y(j))

    for j in range(1, NY):
        y_copy(j).start()

    def rows(core, piece):
        return pl.ds(pl.multiple_of(core * HALF + piece * PIECE, PIECE), PIECE)

    def cols(block):
        return pl.ds(pl.multiple_of(block * 128, 128), 128)

    def w_copy(side, piece):
        return copy(
            w_ref.at[rows(c, piece)], w_out.at[rows(c, piece), cols(x)],
            w_send.at[side, piece], w_recv.at[side, piece], ahead if side == 0 else behind,
        )

    for piece in range(PIECES):
        for side in range(2):
            w_copy(side, piece).start()

    own_w = pltpu.make_async_copy(w_ref, w_out.at[:, cols(x)], local_sem.at[NY])
    own_w.start()

    def z_source(j, start):
        if j == 0:
            return go_ref.at[pl.ds(base + start, 2)]
        return slots.at[j - 1, pl.ds(start, 2)]

    def from_y(j):
        return lax.rem(y - j + NY, NY)

    def z_copy(j, k):
        goal = lax.rem(spot + k, 16)
        core = lax.rem(goal, 2)
        start = goal // 2 * 2 + 2 * core
        return copy(
            z_source(j, start), go_out.at[pl.ds(core, 2), from_y(j), spot],
            z_send.at[j, k - 1], z_recv.at[j, k - 1], ring_z(k),
        )

    def wanted(goal):
        return jnp.logical_or(lax.rem(goal, 2) == 0, lax.rem(goal // 2, 4) != 3)

    keeps = wanted(spot)

    def own_go(j):
        start = z * 2 + 2 * c
        return pltpu.make_async_copy(
            z_source(j, start), go_out.at[pl.ds(c, 2), from_y(j), spot], local_sem.at[j]
        )

    for j in range(NY):
        if j > 0:
            y_copy(j).wait_recv()

        @pl.when(keeps)
        def _():
            own_go(j).start()

        def begin(k, carry):
            @pl.when(wanted(lax.rem(spot + k, 16)))
            def _():
                z_copy(j, k).start()

            return carry

        lax.fori_loop(1, 16, begin, 0)

    def f_copy(piece):
        place_of = w_out.at[rows(c, piece), cols(behind[0])]
        return copy(place_of, place_of, f_send.at[piece], f_recv.at[piece], ahead)

    def s_copy(index, piece):
        block = (behind[0], ahead[0], lax.rem(x + 2, NX))[index]
        place_of = w_out.at[rows(c, piece), cols(block)]
        return copy(place_of, place_of, s_send.at[index, piece], s_recv.at[index, piece], sibling)

    for piece in range(PIECES):
        w_copy(0, piece).wait_recv()
        f_copy(piece).start()
        s_copy(0, piece).start()
        w_copy(1, piece).wait_recv()
        s_copy(1, piece).start()
    for piece in range(PIECES):
        f_copy(piece).wait_recv()
        s_copy(2, piece).start()

    @pl.when(keeps)
    def _():
        for j in range(NY):
            own_go(j).wait()

            def arrive(k, carry):
                source = lax.rem(spot - k + 16, 16)
                landed = go_out.at[pl.ds(c, 2), from_y(j), source]
                copy(landed, landed, z_send.at[j, k - 1], z_recv.at[j, k - 1], ring_z(k)).wait_recv()
                return carry

            lax.fori_loop(1, 16, arrive, 0)

    def e_copy():
        return copy(go_out.at[1], go_out.at[2 * c], e_send, e_recv, sibling)

    whole = lax.rem(z, 4) != 3

    @pl.when(keeps)
    def _():
        e_copy().start()

    @pl.when(jnp.logical_or(c == 1, whole))
    def _():
        e_copy().wait_recv()

    for index in range(3):
        for piece in range(PIECES):
            s_copy(index, piece).wait_recv()

    own_w.wait()
    for j in range(1, NY):
        y_copy(j).wait_send()
    for piece in range(PIECES):
        w_copy(0, piece).wait_send()
        w_copy(1, piece).wait_send()
        f_copy(piece).wait_send()
        for index in range(3):
            s_copy(index, piece).wait_send()

    @pl.when(keeps)
    def _():
        e_copy().wait_send()

    for j in range(NY):

        def leave(k, carry):
            @pl.when(wanted(lax.rem(spot + k, 16)))
            def _():
                z_copy(j, k).wait_send()

            return carry

        lax.fori_loop(1, 16, leave, 0)


def gather_inputs(w_spatial, grad_out):
    anywhere = pl.BlockSpec(memory_space=pl.ANY)
    dma = pltpu.SemaphoreType.DMA
    return pl.pallas_call(
        gather_kernel,
        out_shape=(
            jax.ShapeDtypeStruct((TAP_ROWS, C), BF16),
            jax.ShapeDtypeStruct((3, NY, 16, 8, C), BF16),
            jax.ShapeDtypeStruct((NY - 1, 16, 8, C), BF16),
        ),
        in_specs=[anywhere] * 2,
        out_specs=(anywhere,) * 3,
        scratch_shapes=[
            dma((2, PIECES)), dma((2, PIECES)), dma((PIECES,)), dma((PIECES,)), dma((3, PIECES)), dma((3, PIECES)),
            dma((NY - 1,)), dma((NY - 1,)), dma((NY, 15)), dma((NY, 15)), dma, dma, dma((NY + 1,)),
        ],
        compiler_params=pltpu.CompilerParams(collective_id=0, has_side_effects=True),
        name="gather_inputs",
    )(w_spatial, grad_out)


def group_sum(values):
    lane = lax.broadcasted_iota(jnp.int32, values.shape, 1)
    total = values.shape[1]
    for step in (1, 2, 4, 8):
        upper = lax.rem(lane // step, 2) == 1
        values = values + jnp.where(upper, pltpu.roll(values, step, 1), pltpu.roll(values, total - step, 1))
    return values


def group_mean(full):
    by_chan = jnp.sum(full, axis=0, keepdims=True)
    return group_sum(jnp.broadcast_to(by_chan, (8, C)))[0:1] * (1.0 / (16 * PIX))


def shifted(values):
    col = lax.rem(lax.broadcasted_iota(jnp.int32, (PIX, C), 0), 128)
    before = jnp.where(col == 0, 0.0, pltpu.roll(values, 1, 0))
    after = jnp.where(col == 127, 0.0, pltpu.roll(values, PIX - 1, 0))
    return before.astype(BF16), after.astype(BF16)


def block_kernel(
    x_ref, w_ref, wt_ref, gain_ref, bias_ref, go_ref, gx_ref, p_ref, q_ref, r_ref, xs, gs, acc, time_part
):
    pos = lax.rem(lax.axis_index("wide"), 8)
    edge = jnp.zeros((128, 3 * C), BF16)
    xs[0:128, :] = edge
    xs[640:768, :] = edge
    gs[0:128, :] = edge
    gs[640:768, :] = edge
    before, after = shifted(x_ref[...].astype(F32))
    xs[128:640, 0:C] = before
    xs[128:640, C : 2 * C] = x_ref[...]
    xs[128:640, 2 * C :] = after
    hidden = jnp.zeros((PIX, C), F32)
    for a in range(3):
        hidden = hidden + jnp.dot(
            xs[128 * a : 128 * a + PIX, :], w_ref[1536 * a : 1536 * a + 1536, :], preferred_element_type=F32
        )
    hidden = hidden.astype(BF16).astype(F32)
    gain = gain_ref[...]
    centered = hidden - group_mean(hidden)
    inv_std = lax.rsqrt(group_mean(centered * centered) + EPSILON)
    normed = centered * inv_std
    preact = normed * gain + bias_ref[...]
    sig = jax.nn.sigmoid(preact)
    act = (preact * sig).astype(BF16)

    grad_act = jnp.zeros((PIX, C), F32)
    for k in range(3):
        later = go_ref[k].astype(F32)
        if k > 0:
            later = jnp.where(pos + k < 8, later, 0.0)
        later = later.astype(BF16)
        grad_act = grad_act + lax.dot_general(
            later, wt_ref[C * k : C * k + C, :], CONTRACT_COLS, preferred_element_type=F32
        )
        time_part[:, C * k : C * k + C] = jnp.dot(later.T, act, preferred_element_type=F32)
    grad_act = grad_act.astype(BF16).astype(F32)
    grad_normed = grad_act * sig * (1.0 + preact * (1.0 - sig)) * gain
    grad_hidden = (grad_normed - group_mean(grad_normed) - normed * group_mean(grad_normed * normed)) * inv_std
    grad_low = grad_hidden.astype(BF16)
    before, after = shifted(grad_low.astype(F32))
    gs[128:640, 0:C] = after
    gs[128:640, C : 2 * C] = grad_low
    gs[128:640, 2 * C :] = before
    for a in range(3):
        for b in range(3):
            tap = 3 * a + b
            part = lax.dot_general(
                gs[128 * (2 - a) : 128 * (2 - a) + PIX, C * b : C * b + C],
                w_ref[C * tap : C * tap + C, :],
                CONTRACT_COLS,
                preferred_element_type=F32,
            )
            if tap == 0:
                acc[...] = part
            elif tap < 8:
                acc[...] += part
            else:
                gx_ref[...] = (acc[...] + part).astype(BF16)

    flipped = grad_low.T
    for i in range(NX):
        chunks = []
        for n in range(3 * i, 3 * i + 3):
            a, col = n // 4, 384 * (n % 4)
            chunk = jnp.dot(flipped, xs[128 * a : 128 * a + PIX, col : col + 384], preferred_element_type=F32)
            chunks.append(chunk.reshape(32, 2, 8, 384))
        chunks.append(time_part[:, 384 * i : 384 * i + 384].reshape(32, 2, 8, 384))
        for core in range(2):
            s0, s1, s2, t0 = [chunk[:, core] for chunk in chunks]
            p_ref[core, i] = jnp.concatenate([s0, s1], axis=1).astype(BF16).reshape(NY, NZ, 16, 384)
            rest = jnp.concatenate([s2, t0], axis=1).astype(BF16).reshape(NY, NZ, 16, 384)
            for y in range(NY):
                q_ref[core, y, i] = rest[y, :, :, :256]
                for z in range(NZ):
                    r_ref[core, z, y, i] = rest[y, z, :, 256:]


def block_pass(frames, weights, w_time, gain, bias, later):
    vmem = pl.BlockSpec(memory_space=pltpu.VMEM)
    return pl.pallas_call(
        block_kernel,
        out_shape=(
            jax.ShapeDtypeStruct((PIX, C), BF16),
            jax.ShapeDtypeStruct((2, NX, NY, NZ, 16, 384), BF16),
            jax.ShapeDtypeStruct((2, NY, NX, NZ, 16, 256), BF16),
            jax.ShapeDtypeStruct((2, NZ, NY, NX, 16, 128), BF16),
        ),
        in_specs=[vmem] * 6,
        out_specs=(vmem,) * 4,
        scratch_shapes=[
            pltpu.VMEM((768, 3 * C), BF16),
            pltpu.VMEM((768, 3 * C), BF16),
            pltpu.VMEM((PIX, C), F32),
            pltpu.VMEM((C, 3 * C), F32),
        ],
        compiler_params=pltpu.CompilerParams(vmem_limit_bytes=48 * 1024 * 1024),
        name="block_pass",
    )(frames, weights, w_time, gain, bias, later)


ORDERS = (("x", "y", "z"), ("y", "x", "z"), ("z", "y", "x"))
SIZES = {"x": NX, "y": NY, "z": NZ}
LANES = (384, 256, 128)


def sum_kernel(scale, *refs):
    ins, (spatial_ref, time_ref), refs = refs[:3], refs[3:5], refs[5:]
    x, w, y, z, c = place()
    at = {"x": x, "y": y, "z": z}

    def partner(axis, k):
        moved = dict(at)
        moved[axis] = lax.rem(at[axis] + k, SIZES[axis])
        return (moved["x"], moved["y"] * 16 + moved["z"] * 2 + c)

    sibling = (x, w + 1 - 2 * c)
    greet([sibling] + [partner(axis, k) for axis in "xyz" for k in range(1, SIZES[axis])])

    def copy(src, dst, send, recv, target):
        return pltpu.make_async_remote_copy(
            src_ref=src, dst_ref=dst, send_sem=send, recv_sem=recv, device_id=target, device_id_type=MESH
        )

    class Part:
        pass

    parts = []
    for index in range(3):
        part = Part()
        part.source = ins[index]
        part.order = ORDERS[index]
        (part.pair, part.go1, part.got1, part.sum1, part.go2, part.got2, part.sum2, part.go3, part.got3,
         part.pair_sems, part.sems1, part.sems2, part.sems3) = refs[13 * index : 13 * index + 13]
        part.pair_copy = copy(
            part.source.at[1 - c], part.pair, part.pair_sems.at[0], part.pair_sems.at[1], sibling
        )
        parts.append(part)

    def hop(part, level, k):
        axis = part.order[level]
        sends = (part.go1, part.go2, part.go3)[level]
        lands = (part.got1, part.got2, part.got3)[level]
        sems = (part.sems1, part.sems2, part.sems3)[level]
        goal = lax.rem(at[axis] + k, SIZES[axis])
        return copy(sends.at[goal], lands.at[k - 1], sems.at[0, k - 1], sems.at[1, k - 1], partner(axis, k))

    sequence = (2, 0, 1)
    for index in sequence:
        parts[index].pair_copy.start()
    for index in sequence:
        part = parts[index]
        part.pair_copy.wait_recv()
        axis = part.order[0]
        for k in range(1, SIZES[axis]):
            goal = lax.rem(at[axis] + k, SIZES[axis])
            part.go1[goal] = (part.source[c, goal].astype(F32) + part.pair[goal].astype(F32)).astype(BF16)
            hop(part, 0, k).start()
    for index in (1, 2, 0):
        part = parts[index]
        mine = at[part.order[0]]
        total = part.source[c, mine].astype(F32) + part.pair[mine].astype(F32)
        for k in range(1, SIZES[part.order[0]]):
            hop(part, 0, k).wait_recv()
            total = total + part.got1[k - 1].astype(F32)
        part.sum1[...] = total
        part.go2[...] = total.astype(BF16)
        for k in range(1, SIZES[part.order[1]]):
            hop(part, 1, k).start()
    for index in (1, 2, 0):
        part = parts[index]
        total = part.sum1[at[part.order[1]]]
        for k in range(1, SIZES[part.order[1]]):
            hop(part, 1, k).wait_recv()
            total = total + part.got2[k - 1].astype(F32)
        part.sum2[...] = total
        part.go3[...] = total.astype(BF16)
        for k in range(1, SIZES[part.order[2]]):
            hop(part, 2, k).start()
    results = [None] * 3
    for index in (1, 2, 0):
        part = parts[index]
        total = part.sum2[at[part.order[2]]]
        for k in range(1, SIZES[part.order[2]]):
            hop(part, 2, k).wait_recv()
            total = total + part.got3[k - 1].astype(F32)
        results[index] = total * scale
    first, second, third = results
    spatial_ref[:, 0:384] = first[0:8]
    spatial_ref[:, 384:768] = first[8:16]
    spatial_ref[:, 768:1024] = second[0:8]
    spatial_ref[:, 1024:1152] = third[0:8]
    time_ref[:, 0:256] = second[8:16]
    time_ref[:, 256:384] = third[8:16]
    for part in parts:
        part.pair_copy.wait_send()
        for level in range(3):
            for k in range(1, SIZES[part.order[level]]):
                hop(part, level, k).wait_send()


def sum_partials(parts, scale):
    vmem = pl.BlockSpec(memory_space=pltpu.VMEM)
    dma = pltpu.SemaphoreType.DMA
    scratch = []
    for order, lanes in zip(ORDERS, LANES):
        n1, n2, n3 = [SIZES[axis] for axis in order]
        scratch += [
            pltpu.VMEM((n1, n2, n3, 16, lanes), BF16),
            pltpu.VMEM((n1, n2, n3, 16, lanes), BF16),
            pltpu.VMEM((n1 - 1, n2, n3, 16, lanes), BF16),
            pltpu.VMEM((n2, n3, 16, lanes), F32),
            pltpu.VMEM((n2, n3, 16, lanes), BF16),
            pltpu.VMEM((n2 - 1, n3, 16, lanes), BF16),
            pltpu.VMEM((n3, 16, lanes), F32),
            pltpu.VMEM((n3, 16, lanes), BF16),
            pltpu.VMEM((n3 - 1, 16, lanes), BF16),
            dma((2,)),
            dma((2, n1 - 1)),
            dma((2, n2 - 1)),
            dma((2, n3 - 1)),
        ]

    def kernel(*refs):
        sum_kernel(scale, *refs)

    return pl.pallas_call(
        kernel,
        out_shape=(jax.ShapeDtypeStruct((8, 1152), F32), jax.ShapeDtypeStruct((8, 384), F32)),
        in_specs=[vmem] * 3,
        out_specs=(vmem,) * 2,
        scratch_shapes=scratch,
        compiler_params=pltpu.CompilerParams(
            collective_id=1, has_side_effects=True, vmem_limit_bytes=48 * 1024 * 1024
        ),
        name="sum_partials",
    )(*parts)


def shards(clips, w_spatial, w_time, norm_gain, norm_bias, grad_out):
    weights, later, _ = gather_inputs(w_spatial, grad_out.reshape(64, 8, C))
    grad_clips, *partials = block_pass(
        clips.reshape(PIX, C),
        weights,
        w_time,
        norm_gain.reshape(1, C),
        norm_bias.reshape(1, C),
        later.reshape(3, PIX, C),
    )
    scale = float(PIX * 64 * NX) ** (-0.5)
    spatial, time = sum_partials(partials, scale)
    return grad_clips.reshape(clips.shape), spatial.T, time.T


def solution(mesh):
    return jax.shard_map(
        shards,
        mesh=mesh,
        in_specs=(
            P("dp", "wide", None, None, None),
            P(None, "dp"),
            P(),
            P(),
            P(),
            P("dp", None, "wide", None),
        ),
        out_specs=(P("dp", "wide", None, None, None), P("dp", "wide"), P("dp", "wide")),
        check_vma=False,
    )
```

```python
import jax
import jax.numpy as jnp
from jax import lax
from jax.experimental import pallas as pl
from jax.experimental.pallas import tpu as pltpu
from jax.sharding import PartitionSpec as P

MESH = pl.DeviceIdType.MESH
F32 = jnp.float32
BF16 = jnp.bfloat16
EPSILON = 1e-06
CONTRACT_COLS = (((1,), (1,)), ((), ()))
NX, NY, NZ = 4, 4, 8
C = 512
PIX = 512
TAP_ROWS = 4608
PIECES = 3
PIECE = TAP_ROWS // PIECES // 2
SIZES = {"x": NX, "y": NY, "z": NZ}
ORDERS = (("x", "y", "z"), ("y", "x", "z"), ("z", "y", "x"))
LANES = (384, 256, 128)


def place():
    x = lax.axis_index("dp")
    w = lax.axis_index("wide")
    return x, w, w // 16, (w // 2) % 8, w % 2


def greet(partners):
    barrier = pltpu.get_barrier_semaphore()
    for partner in partners:
        pl.semaphore_signal(barrier, inc=1, device_id=partner, device_id_type=MESH)
    pl.semaphore_wait(barrier, len(partners))


def group_sum(values):
    lane = lax.broadcasted_iota(jnp.int32, values.shape, 1)
    total = values.shape[1]
    for step in (1, 2, 4, 8):
        upper = lax.rem(lane // step, 2) == 1
        values = values + jnp.where(upper, pltpu.roll(values, step, 1), pltpu.roll(values, total - step, 1))
    return values


def group_mean(full):
    by_chan = jnp.sum(full, axis=0, keepdims=True)
    return group_sum(jnp.broadcast_to(by_chan, (8, C)))[0:1] * (1.0 / (16 * PIX))


def shifted(values):
    col = lax.rem(lax.broadcasted_iota(jnp.int32, (PIX, C), 0), 128)
    before = jnp.where(col == 0, 0.0, pltpu.roll(values, 1, 0))
    after = jnp.where(col == 127, 0.0, pltpu.roll(values, PIX - 1, 0))
    return before.astype(BF16), after.astype(BF16)


def copy(src, dst, send, recv, target):
    return pltpu.make_async_remote_copy(
        src_ref=src, dst_ref=dst, send_sem=send, recv_sem=recv, device_id=target, device_id_type=MESH
    )


def own_rows(values, core):
    split = values.reshape(32, 2, 8, values.shape[1])
    return jnp.where(core == 0, split[:, 0], split[:, 1]).reshape(256, values.shape[1]).astype(BF16)


class Part:
    pass


def block_kernel(scale, *refs):
    (x_ref, w_ref, wt_ref, gain_ref, bias_ref, go_ref, gx_ref, spatial_ref, time_ref) = refs[:9]
    (weights, w_time, frames, windows, grad_windows, landed, slots, later, later_rows, acts, grads, grad_rows, acc,
     time_part, gx_low) = refs[9:24]
    (w_send, w_recv, f_send, f_recv, s_send, s_recv, y_send, y_recv, z_send, z_recv, e_sems, pair_sems,
     local_sem) = refs[24:37]
    part_refs = refs[37:]

    x, w, y, z, c = place()
    at = {"x": x, "y": y, "z": z}
    way = 1 - 2 * c
    sibling = (x, w + way)
    ahead = (lax.rem(x + way + NX, NX), w)
    behind = (lax.rem(x - way + NX, NX), w)
    base = y * 16
    spot = lax.rem(w, 16)

    def partner(axis, k):
        moved = dict(at)
        moved[axis] = lax.rem(at[axis] + k, SIZES[axis])
        return (moved["x"], moved["y"] * 16 + moved["z"] * 2 + c)

    def ring_y(j):
        return partner("y", j)

    def ring_z(k):
        return (x, base + lax.rem(spot + k, 16))

    loads = [
        pltpu.make_async_copy(x_ref, frames.at[c], local_sem.at[5]),
        pltpu.make_async_copy(wt_ref, w_time, local_sem.at[6]),
    ]
    for load in loads:
        load.start()
    greet(
        [partner("x", k) for k in range(1, NX)]
        + [ring_y(j) for j in range(1, NY)]
        + [ring_z(k) for k in range(1, 16)]
    )

    def rows(core, piece):
        return pl.ds(pl.multiple_of((2 * piece + core) * PIECE, PIECE), PIECE)

    def cols(block):
        return pl.ds(pl.multiple_of(block * 128, 128), 128)

    def w_copy(side, piece):
        return copy(
            w_ref.at[rows(c, piece)], weights.at[rows(c, piece), cols(x)],
            w_send.at[side, piece], w_recv.at[side, piece], ahead if side == 0 else behind,
        )

    def f_copy(piece):
        spot_of = weights.at[rows(c, piece), cols(behind[0])]
        return copy(spot_of, spot_of, f_send.at[piece], f_recv.at[piece], ahead)

    def s_copy(index, piece):
        block = (behind[0], ahead[0], lax.rem(x + 2, NX))[index]
        spot_of = weights.at[rows(c, piece), cols(block)]
        return copy(spot_of, spot_of, s_send.at[index, piece], s_recv.at[index, piece], sibling)

    def y_copy(j):
        source = pl.ds(lax.rem(y + j, NY) * 16, 16)
        return copy(go_ref.at[source], slots.at[j - 1], y_send.at[j - 1], y_recv.at[j - 1], ring_y(j))

    def z_source(j, start):
        if j == 0:
            return go_ref.at[pl.ds(base + start, 2)]
        return slots.at[j - 1, pl.ds(start, 2)]

    def from_y(j):
        return lax.rem(y - j + NY, NY)

    def z_copy(j, k):
        goal = lax.rem(spot + k, 16)
        core = lax.rem(goal, 2)
        start = goal // 2 * 2 + 2 * core
        return copy(
            z_source(j, start), landed.at[pl.ds(2 * core, 2), from_y(j), spot],
            z_send.at[j, k - 1], z_recv.at[j, k - 1], ring_z(k),
        )

    def wanted(goal):
        return jnp.logical_or(lax.rem(goal, 2) == 0, lax.rem(goal // 2, 4) != 3)

    keeps = wanted(spot)
    whole = lax.rem(z, 4) != 3

    def own_go(j):
        start = z * 2 + 2 * c
        return pltpu.make_async_copy(
            z_source(j, start), landed.at[pl.ds(2 * c, 2), from_y(j), spot], local_sem.at[j]
        )

    def z_start(j):
        if j > 0:
            y_copy(j).wait_recv()

        @pl.when(keeps)
        def _():
            own_go(j).start()

        def begin(k, carry):
            @pl.when(wanted(lax.rem(spot + k, 16)))
            def _():
                z_copy(j, k).start()

            return carry

        lax.fori_loop(1, 16, begin, 0)

    def pair_copy(index, array):
        return copy(array.at[c], array.at[c], pair_sems.at[0, index], pair_sems.at[1, index], sibling)

    for piece in range(PIECES):
        for side in range(2):
            w_copy(side, piece).start()
    for j in (2, 1, 3):
        y_copy(j).start()
    z_start(0)
    own_w = pltpu.make_async_copy(w_ref, weights.at[:, cols(x)], local_sem.at[4])
    own_w.start()
    loads[0].wait()
    pair_copy(0, frames).start()
    edge = jnp.zeros((128, 3 * C), BF16)

    def fill(target, values, low, flip):
        before, after = shifted(values)
        target[0:128, :] = edge
        target[640:768, :] = edge
        target[128:640, 0:C] = after if flip else before
        target[128:640, C : 2 * C] = low
        target[128:640, 2 * C :] = before if flip else after

    fill(windows.at[c], frames[c].astype(F32), frames[c], False)
    w_copy(0, 0).wait_recv()
    f_copy(0).start()
    s_copy(0, 0).start()
    w_copy(1, 0).wait_recv()
    s_copy(1, 0).start()
    z_start(1)
    z_start(3)
    for piece in range(1, PIECES):
        w_copy(0, piece).wait_recv()
        f_copy(piece).start()
        s_copy(0, piece).start()
        w_copy(1, piece).wait_recv()
        s_copy(1, piece).start()
        if piece == 1:
            z_start(2)
    own_w.wait()

    def forward(a):
        for index in range(3):
            s_copy(index, a).wait_recv()
        part = jnp.dot(
            windows[c, 128 * a : 128 * a + PIX, :], weights[1536 * a : 1536 * a + 1536, :], preferred_element_type=F32
        )
        if a == 0:
            acc[...] = part
        else:
            acc[...] += part

    for piece in range(PIECES):
        f_copy(piece).wait_recv()
        s_copy(2, piece).start()
        if piece > 0:
            forward(piece - 1)
    forward(PIECES - 1)
    hidden = acc[...].astype(BF16).astype(F32)
    gain = gain_ref[...]
    centered = hidden - group_mean(hidden)
    inv_std = lax.rsqrt(group_mean(centered * centered) + EPSILON)
    normed = centered * inv_std
    preact = normed * gain + bias_ref[...]
    sig = jax.nn.sigmoid(preact)
    acts[c] = (preact * sig).astype(BF16)
    pair_copy(1, acts).start()
    slope = sig * (1.0 + preact * (1.0 - sig)) * gain

    pair_copy(0, frames).wait_recv()
    fill(windows.at[1 - c], frames[1 - c].astype(F32), frames[1 - c], False)

    @pl.when(keeps)
    def _():
        for j in range(NY):
            own_go(j).wait()

            def arrive(k, carry):
                source = lax.rem(spot - k + 16, 16)
                place_of = landed.at[pl.ds(2 * c, 2), from_y(j), source]
                copy(place_of, place_of, z_send.at[j, k - 1], z_recv.at[j, k - 1], ring_z(k)).wait_recv()
                return carry

            lax.fori_loop(1, 16, arrive, 0)

    def e_copy():
        both = landed.at[pl.ds(2 * c, 2)]
        return copy(both, both, e_sems.at[0], e_sems.at[1], sibling)

    @pl.when(keeps)
    def _():
        e_copy().start()

    @pl.when(jnp.logical_or(c == 1, whole))
    def _():
        e_copy().wait_recv()

    for j in range(4):

        def take():
            later[j] = landed[j].astype(F32).reshape(PIX, C).astype(BF16)

        if j < 2:
            take()
        else:
            pl.when(whole)(take)

            @pl.when(jnp.logical_not(whole))
            def _():
                later[j] = jnp.zeros((PIX, C), BF16)

    loads[1].wait()
    grad_act = jnp.zeros((PIX, C), F32)
    for k in range(3):
        grad_act = grad_act + lax.dot_general(
            later[c + k], w_time[C * k : C * k + C, :], CONTRACT_COLS, preferred_element_type=F32
        )
    grad_normed = grad_act.astype(BF16).astype(F32) * slope
    grad_hidden = (grad_normed - group_mean(grad_normed) - normed * group_mean(grad_normed * normed)) * inv_std
    grad_low = grad_hidden.astype(BF16)
    grads[c] = grad_low
    pair_copy(2, grads).start()

    for j in range(4):
        later_rows[j] = own_rows(later[j].astype(F32).T, c)
    pair_copy(1, acts).wait_recv()
    for k in range(3):
        time_part[:, C * k : C * k + C] = jnp.dot(
            later_rows[k], acts[0], preferred_element_type=F32
        ) + jnp.dot(later_rows[k + 1], acts[1], preferred_element_type=F32)

    parts = []
    for index in range(3):
        part = Part()
        part.order = ORDERS[index]
        if index < 2:
            (part.data, part.land_a, part.go_b, part.land_b, part.sum1, part.go2, part.got2, part.sum2, part.go3,
             part.got3, part.sems1, part.sems2, part.sems3) = part_refs[13 * index : 13 * index + 13]
        else:
            (part.data, part.got1, part.sum1, part.go2, part.got2, part.sum2, part.go3,
             part.got3, part.sems1, part.sems2, part.sems3) = part_refs[26:37]
        parts.append(part)
    ring_p, ring_q, direct = parts

    def hop(part, level, k):
        axis = part.order[level]
        sends = (part.data, part.go2, part.go3)[level]
        lands = (None if part is not direct else part.got1, part.got2, part.got3)[level]
        sems = (part.sems1, part.sems2, part.sems3)[level]
        goal = lax.rem(at[axis] + k, SIZES[axis])
        return copy(sends.at[goal], lands.at[k - 1], sems.at[0, k - 1], sems.at[1, k - 1], partner(axis, k))

    def ring_hop(part, stage, d):
        axis = part.order[0]
        goal = lax.rem(at[axis] + (1, 3)[d], 4)
        far = lax.rem(at[axis] + 2, 4)
        half = pl.ds(2 * d, 2)
        other = pl.ds(2 - 2 * d, 2)
        src, dst = (
            (part.data.at[far, half], part.land_a.at[d]),
            (part.data.at[goal, other], part.land_b.at[d, other]),
            (part.go_b.at[d], part.land_b.at[d, half]),
        )[stage]
        return copy(src, dst, part.sems1.at[0, stage, d], part.sems1.at[1, stage, d], partner(axis, (1, 3)[d]))

    def time_cols(i, start, size):
        return time_part[:, pl.ds(pl.multiple_of(384 * i + start, 128), size)].reshape(32, 8, size)

    for i in range(NX):
        rest = jnp.concatenate([time_cols(i, 0, 128), time_cols(i, 128, 128)], axis=1).astype(BF16)
        rest = rest.reshape(NY, NZ, 16, 128)
        for zz in range(NZ):
            direct.data[zz, :, i] = rest[:, zz]
    for k in range(1, NZ):
        hop(direct, 0, k).start()

    grad_rows[c] = own_rows(grads[c].astype(F32).T, c)
    pair_copy(2, grads).wait_recv()
    grad_rows[1 - c] = own_rows(grads[1 - c].astype(F32).T, c)

    def spatial(i, ch):
        n = 3 * i + ch
        a = n // 4
        top = pl.ds(pl.multiple_of(128 * a, 128), PIX)
        side = pl.ds(pl.multiple_of(384 * lax.rem(n, 4), 128), 384)
        total = jnp.dot(grad_rows[0], windows[0, top, side], preferred_element_type=F32) + jnp.dot(
            grad_rows[1], windows[1, top, side], preferred_element_type=F32
        )
        return total.reshape(32, 8, 384)

    for j in (2, 1, 3, 0):
        i = lax.rem(x + j, NX)
        s0, s1, s2 = [spatial(i, ch) for ch in range(3)]
        ring_p.data[i] = jnp.concatenate([s0, s1], axis=1).astype(BF16).reshape(NY, NZ, 16, 384)
        tail = jnp.concatenate([s2[:, :, 256:], time_cols(i, 256, 128)], axis=2)
        mixed = jnp.concatenate([s2[:, :, :256], tail], axis=1).astype(BF16).reshape(NY, NZ, 16, 256)
        for yy in range(NY):
            ring_q.data[yy, i] = mixed[yy]
        if j == 2:
            ring_hop(ring_p, 0, 0).start()
            ring_hop(ring_p, 0, 1).start()
        elif j == 1:
            ring_hop(ring_p, 1, 0).start()
        elif j == 3:
            ring_hop(ring_p, 1, 1).start()
    for stage in range(2):
        for d in range(2):
            ring_hop(ring_q, stage, d).start()

    fill(grad_windows, grads[c].astype(F32), grads[c], True)

    def backward(a):
        for b in range(3):
            tap = 3 * a + b
            part = lax.dot_general(
                grad_windows[128 * (2 - a) : 128 * (2 - a) + PIX, C * b : C * b + C],
                weights[C * tap : C * tap + C, :],
                CONTRACT_COLS,
                preferred_element_type=F32,
            )
            if tap == 0:
                acc[...] = part
            else:
                acc[...] += part

    def relay(part):
        axis = part.order[0]
        for d in range(2):
            goal = lax.rem(at[axis] + (1, 3)[d], 4)
            ring_hop(part, 0, d).wait_recv()
            part.go_b[d] = (
                part.data[goal, 2 * d : 2 * d + 2].astype(F32) + part.land_a[d].astype(F32)
            ).astype(BF16)
            ring_hop(part, 2, d).start()

    backward(0)
    relay(ring_p)
    relay(ring_q)
    backward(1)
    backward(2)
    gx_low[...] = acc[...].astype(BF16)
    gx_out = pltpu.make_async_copy(gx_low, gx_ref, local_sem.at[7])
    gx_out.start()

    def second(part, total):
        part.sum1[...] = total
        part.go2[...] = total.astype(BF16)
        for k in range(1, SIZES[part.order[1]]):
            hop(part, 1, k).start()

    def ring_total(part):
        for stage in (1, 2):
            for d in range(2):
                ring_hop(part, stage, d).wait_recv()
        mine = at[part.order[0]]
        return part.data[mine].astype(F32) + part.land_b[0].astype(F32) + part.land_b[1].astype(F32)

    second(ring_q, ring_total(ring_q))
    second(ring_p, ring_total(ring_p))
    total = direct.data[z].astype(F32)
    for k in range(1, NZ):
        hop(direct, 0, k).wait_recv()
        total = total + direct.got1[k - 1].astype(F32)
    second(direct, total)
    for part in (ring_q, ring_p, direct):
        total = part.sum1[at[part.order[1]]]
        for k in range(1, SIZES[part.order[1]]):
            hop(part, 1, k).wait_recv()
            total = total + part.got2[k - 1].astype(F32)
        part.sum2[...] = total
        part.go3[...] = total.astype(BF16)
        for k in range(1, SIZES[part.order[2]]):
            hop(part, 2, k).start()
    results = []
    for part in (ring_q, ring_p, direct):
        total = part.sum2[at[part.order[2]]]
        for k in range(1, SIZES[part.order[2]]):
            hop(part, 2, k).wait_recv()
            total = total + part.got3[k - 1].astype(F32)
        results.append(total * scale)
    mixed, first, last = results
    spatial_ref[:, 0:384] = first[0:8]
    spatial_ref[:, 384:768] = first[8:16]
    spatial_ref[:, 768:1024] = mixed[0:8]
    spatial_ref[:, 1024:1152] = mixed[8:16, 0:128]
    time_ref[:, 0:128] = last[0:8]
    time_ref[:, 128:256] = last[8:16]
    time_ref[:, 256:384] = mixed[8:16, 128:256]

    gx_out.wait()
    for j in range(1, NY):
        y_copy(j).wait_send()
    for piece in range(PIECES):
        w_copy(0, piece).wait_send()
        w_copy(1, piece).wait_send()
        f_copy(piece).wait_send()
        for index in range(3):
            s_copy(index, piece).wait_send()
    pair_copy(0, frames).wait_send()
    pair_copy(1, acts).wait_send()
    pair_copy(2, grads).wait_send()

    @pl.when(keeps)
    def _():
        e_copy().wait_send()

    for j in range(NY):

        def leave(k, carry):
            @pl.when(wanted(lax.rem(spot + k, 16)))
            def _():
                z_copy(j, k).wait_send()

            return carry

        lax.fori_loop(1, 16, leave, 0)
    for part in parts:
        if part is direct:
            for k in range(1, NZ):
                hop(part, 0, k).wait_send()
        else:
            for stage in range(3):
                for d in range(2):
                    ring_hop(part, stage, d).wait_send()
        for level in (1, 2):
            for k in range(1, SIZES[part.order[level]]):
                hop(part, level, k).wait_send()


def block_pass(frames, w_spatial, w_time, gain, bias, grad_out, scale):
    vmem = pl.BlockSpec(memory_space=pltpu.VMEM)
    anywhere = pl.BlockSpec(memory_space=pl.ANY)
    dma = pltpu.SemaphoreType.DMA
    scratch = [
        pltpu.VMEM((TAP_ROWS, C), BF16),
        pltpu.VMEM((3 * C, C), BF16),
        pltpu.VMEM((2, PIX, C), BF16),
        pltpu.VMEM((2, 768, 3 * C), BF16),
        pltpu.VMEM((768, 3 * C), BF16),
        pltpu.VMEM((4, NY, 16, 8, C), BF16),
        pltpu.VMEM((NY - 1, 16, 8, C), BF16),
        pltpu.VMEM((4, PIX, C), BF16),
        pltpu.VMEM((4, 256, PIX), BF16),
        pltpu.VMEM((2, PIX, C), BF16),
        pltpu.VMEM((2, PIX, C), BF16),
        pltpu.VMEM((2, 256, PIX), BF16),
        pltpu.VMEM((PIX, C), F32),
        pltpu.VMEM((256, 3 * C), F32),
        pltpu.VMEM((PIX, C), BF16),
        dma((2, PIECES)), dma((2, PIECES)), dma((PIECES,)), dma((PIECES,)), dma((3, PIECES)), dma((3, PIECES)),
        dma((NY - 1,)), dma((NY - 1,)), dma((NY, 15)), dma((NY, 15)), dma((2,)), dma((2, 3)), dma((8,)),
    ]
    for order, lanes in zip(ORDERS, LANES):
        n1, n2, n3 = [SIZES[axis] for axis in order]
        scratch.append(pltpu.VMEM((n1, n2, n3, 16, lanes), BF16))
        if n1 == 4:
            scratch += [
                pltpu.VMEM((2, 2, n3, 16, lanes), BF16),
                pltpu.VMEM((2, 2, n3, 16, lanes), BF16),
                pltpu.VMEM((2, 4, n3, 16, lanes), BF16),
            ]
        else:
            scratch.append(pltpu.VMEM((n1 - 1, n2, n3, 16, lanes), BF16))
        scratch += [
            pltpu.VMEM((n2, n3, 16, lanes), F32),
            pltpu.VMEM((n2, n3, 16, lanes), BF16),
            pltpu.VMEM((n2 - 1, n3, 16, lanes), BF16),
            pltpu.VMEM((n3, 16, lanes), F32),
            pltpu.VMEM((n3, 16, lanes), BF16),
            pltpu.VMEM((n3 - 1, 16, lanes), BF16),
            dma((2, 3, 2)) if n1 == 4 else dma((2, n1 - 1)),
            dma((2, n2 - 1)),
            dma((2, n3 - 1)),
        ]

    def kernel(*refs):
        block_kernel(scale, *refs)

    return pl.pallas_call(
        kernel,
        out_shape=(
            jax.ShapeDtypeStruct((PIX, C), BF16),
            jax.ShapeDtypeStruct((8, 1152), F32),
            jax.ShapeDtypeStruct((8, 384), F32),
        ),
        in_specs=[anywhere] * 3 + [vmem] * 2 + [anywhere],
        out_specs=(anywhere, vmem, vmem),
        scratch_shapes=scratch,
        compiler_params=pltpu.CompilerParams(
            collective_id=0, has_side_effects=True, vmem_limit_bytes=58 * 1024 * 1024
        ),
        name="block_pass",
    )(frames, w_spatial, w_time, gain, bias, grad_out)


def shards(clips, w_spatial, w_time, norm_gain, norm_bias, grad_out):
    scale = float(PIX * 64 * NX) ** (-0.5)
    grad_clips, spatial, time = block_pass(
        clips.reshape(PIX, C),
        w_spatial,
        w_time,
        norm_gain.reshape(1, C),
        norm_bias.reshape(1, C),
        grad_out.reshape(64, 8, C),
        scale,
    )
    return grad_clips.reshape(clips.shape), spatial.T, time.T


def solution(mesh):
    return jax.shard_map(
        shards,
        mesh=mesh,
        in_specs=(
            P("dp", "wide", None, None, None),
            P(None, "dp"),
            P(),
            P(),
            P(),
            P("dp", None, "wide", None),
        ),
        out_specs=(P("dp", "wide", None, None, None), P("dp", "wide"), P("dp", "wide")),
        check_vma=False,
    )
```
